256 devices in a mesh: wide: 128 (over x, y, z), narrow: 2 (over core).
Axes of the slice: x: 4, y: 4, z: 8, core: 2. Of those that a mesh axis runs over, the one named last changes fastest.
Arguments:
- spectra: bfloat16 [1015808, 256], P('wide'), may hold values from -6 to 6
- legendre: bfloat16 [1015808, 1024], P('wide', 'narrow'), may hold values from -0.09375 to 0.09375
- weights: float32 [2, 512], P('narrow', 'wide'), may hold values from 0.5 to 5
- coefficient: float32 [2, 512, 2, 511], P('narrow', 'wide')
- row_length: int32 [2, 512], P('narrow', 'wide'), may hold values from 1 to 256, as said below
- wave_number: int32 [256], P('wide'), may hold values from 0 to 255, as said below
Outputs:
- spectra_out: bfloat16 [1015808, 256], P(('wide', 'narrow'))
The draws below stay inside these ranges and needn't reach their ends.
Inputs may be any that keep to these rules, and one draw needn't show every extreme that they name: `wave_number`: a permutation of the band; entries 2 i and 2 i + 1 sum to 255. `row_length`: some latitude row resolves all 256.
All inputs are finite; a program needn't handle non-finite values.
Results may differ from the reference program's by a relative error of at most 0.0063.
Values may be sent and summed in bfloat16 or wider, within the bound.
A program may use at most 128 MiB of HBM per device.

```python
import math
import jax
import jax.numpy as jnp
from jax import lax

TRUNC = 3999
M = 256
ROWS = 1015808
F2 = 256
LATQ = 512
NLAT = 1024
HARM = 511
N_NARROW = 2


def draw_wave_number(key, part):
    key = jax.random.fold_in(key, 11)
    order = jax.random.permutation(key, M // 2).astype(jnp.int32)
    return jnp.stack([order, M - 1 - order], axis=1).reshape(M)


def draw_row_length(key, part):
    key = jax.random.fold_in(key, 12)
    first_key, second_key = jax.random.split(key)
    lengths = jax.random.randint(first_key, (NLAT,), 1, M + 1).astype(jnp.int32)
    target = jax.random.randint(second_key, (), 0, NLAT).astype(jnp.int32)
    places = jnp.arange(NLAT, dtype=jnp.int32)
    lengths = jnp.where(places == target, M, lengths)
    return lengths.reshape(NLAT // LATQ, LATQ)


def draw_coefficient(key, part):
    key = jax.random.fold_in(key, 13)
    first_key, second_key = jax.random.split(key)
    spread = 0.5 / M ** 0.5
    base = jax.random.normal(first_key, (NLAT, 2, HARM), jnp.float32) * spread
    centre = jax.random.uniform(second_key, (NLAT,), jnp.float32, 0.8, 1.2)
    places = jnp.arange(HARM, dtype=jnp.int32)
    parts = jnp.arange(2, dtype=jnp.int32)
    spot = ((places[None, :] == M - 1) & (parts[:, None] == 0)).astype(jnp.float32)
    values = base + centre[:, None, None] * spot[None, :, :]
    return values.reshape(NLAT // LATQ, LATQ, 2, HARM)


def level_of(stream_key, dims, cuts, smallest, largest):
    loudness, own = 1.0, jax.random.fold_in(stream_key, 6)
    for position, shards_of in cuts:
        heights = jnp.exp(jax.random.uniform(jax.random.fold_in(own, position), (shards_of,), jnp.float32, smallest / len(cuts), largest / len(cuts)))
        loudness = loudness * jnp.repeat(heights, dims[position] // shards_of).reshape([-1 if axis == position else 1 for axis in range(len(dims))])
    return loudness


def gaussian(own_key, extent, scale, limit, shards=(), kind=jnp.bfloat16):
    level = level_of(own_key, extent, shards, -0.22, 0.18) if shards else 1.0
    values = jax.random.normal(own_key, extent, jnp.float32) * scale * level
    return jnp.minimum(jnp.maximum(values, -limit), limit).astype(kind)


def setup_inputs(seed: int = 0) -> dict:
    arg_keys = jax.random.split(jax.random.key(seed), 7)
    spectra = gaussian(arg_keys[0], (ROWS, F2), 1.0, 6.0, ((0, 128),))
    legendre = gaussian(arg_keys[1], (ROWS, NLAT), TRUNC ** -0.5, 0.09375, ((0, 128), (1, 2)))
    weights = jnp.clip(jnp.exp(math.log(5.0) - 2.3025851 * jax.random.uniform(arg_keys[2], (N_NARROW, LATQ), jnp.float32) ** level_of(arg_keys[2], (N_NARROW, LATQ), ((0, 2), (1, 128)), -0.2, 0.2)), 0.5, 5.0)
    coefficient = draw_coefficient(jax.random.fold_in(arg_keys[6], 71), 0)
    row_length = draw_row_length(jax.random.fold_in(arg_keys[6], 71), 0)
    wave_number = draw_wave_number(jax.random.fold_in(arg_keys[6], 71), 0)
    return dict(spectra=spectra, legendre=legendre, weights=weights, coefficient=coefficient, row_length=row_length, wave_number=wave_number)


def column_product(left_rows, right_rows):
    return jnp.dot(left_rows.T, right_rows, preferred_element_type=jnp.float32)


def reference(spectra, legendre, weights, coefficient, row_length, wave_number):
    band_size = wave_number.shape[0]
    pair_count = band_size // 2
    pack_rows = spectra.shape[0] // pair_count
    columns = spectra.shape[1]
    half_cols = columns // 2
    lat_count = legendre.shape[1]
    lower_end = TRUNC + 2 - band_size
    upper_end = TRUNC + 1
    total_rows = 2 * TRUNC + 3 - band_size
    spectra_pairs = spectra.reshape(pair_count, pack_rows, columns)
    legendre_pairs = legendre.reshape(pair_count, pack_rows, lat_count)
    first_waves = wave_number.reshape(pair_count, 2)[:, 0]
    offsets = lower_end + jnp.arange(upper_end - lower_end, dtype=jnp.int32)

    def inverse(operands):
        rows_here, table, first = operands
        in_first = (offsets < TRUNC + 1 - first)[:, None]
        middle_rows = rows_here[lower_end:upper_end]
        zero_rows = jnp.zeros_like(middle_rows)
        middle_first = jnp.where(in_first, middle_rows, zero_rows)
        middle_second = jnp.where(in_first, zero_rows, middle_rows)
        middle_table = table[lower_end:upper_end]
        first_wave = column_product(table[:lower_end], rows_here[:lower_end]) + column_product(middle_table, middle_first)
        second_wave = column_product(table[upper_end:total_rows], rows_here[upper_end:total_rows]) + column_product(middle_table, middle_second)
        return jnp.stack([first_wave, second_wave]).astype(jnp.bfloat16)

    fourier = lax.map(inverse, (spectra_pairs, legendre_pairs, first_waves))
    fourier = fourier.reshape(band_size, lat_count, columns)
    by_latitude = jnp.transpose(fourier, (1, 0, 2))
    coef_rows = coefficient.reshape(lat_count, 2, 2 * band_size - 1)
    lengths = row_length.reshape(lat_count)
    gauss = weights.reshape(lat_count)
    harmonic = wave_number[:, None] - wave_number[None, :] + band_size - 1

    def couple(operands):
        values, coef, length, weight = operands
        coupling_real = coef[0][harmonic].astype(jnp.bfloat16)
        coupling_imag = coef[1][harmonic].astype(jnp.bfloat16)
        resolved = (wave_number < length)[:, None]
        masked = jnp.where(resolved, values, jnp.zeros_like(values))
        real_part = jnp.dot(coupling_real, masked, preferred_element_type=jnp.float32)
        imag_part = jnp.dot(coupling_imag, masked, preferred_element_type=jnp.float32)
        coupled = jnp.concatenate([real_part[:, :half_cols] - imag_part[:, half_cols:], real_part[:, half_cols:] + imag_part[:, :half_cols]], axis=1)
        scaled = coupled * weight
        return jnp.where(resolved, scaled, jnp.zeros_like(scaled)).astype(jnp.bfloat16)

    returned = lax.map(couple, (by_latitude, coef_rows, lengths, gauss))
    back = jnp.transpose(returned, (1, 0, 2)).reshape(pair_count, 2, lat_count, columns)

    def direct(operands):
        table, waves, first = operands
        in_first = (offsets < TRUNC + 1 - first)[:, None]
        middle_table = table[lower_end:upper_end]
        top_rows = jnp.dot(table[:lower_end], waves[0], preferred_element_type=jnp.float32)
        middle_out = jnp.where(in_first, jnp.dot(middle_table, waves[0], preferred_element_type=jnp.float32), jnp.dot(middle_table, waves[1], preferred_element_type=jnp.float32))
        bottom = jnp.dot(table[upper_end:total_rows], waves[1], preferred_element_type=jnp.float32)
        padding = jnp.zeros((pack_rows - total_rows, columns), jnp.float32)
        return jnp.concatenate([top_rows, middle_out, bottom, padding], axis=0).astype(jnp.bfloat16)

    result = lax.map(direct, (legendre_pairs, back, first_waves))
    return result.reshape(pair_count * pack_rows, columns)
```

```python
import functools

import jax
import jax.numpy as jnp
from jax import lax
from jax.experimental import pallas as pl
from jax.experimental.pallas import tpu as pltpu
from jax.sharding import PartitionSpec as P

TRUNC = 3999
NX, NY, NZ = 4, 4, 8
CHIPS = NX * NY * NZ
BAND = 2 * CHIPS
MIDDLE = 3744
UPPER = TRUNC + 1
TOTAL = 2 * TRUNC + 3 - BAND
SPAN = 4016
ROWS = MIDDLE + SPAN
SHARE = 3968
BLOCK = 416
MESH = pl.DeviceIdType.MESH
BF16, F32 = jnp.bfloat16, jnp.float32
ROW_ROW = (((0,), (0,)), ((), ()))


def rows_iota(shape):
    return lax.broadcasted_iota(jnp.int32, shape, 0)


def kernel(
    spectra, legendre, weights, coef, lengths, waves, out,
    leg, spec_a, spec_b, leg_x, send, recv, send_back, recv_back, grid, harm, table,
    block_z, from_z, block_y, from_y, block_x, from_x, rows, rows_x, acc, mid, mid_x,
    load_sem, send_sem, recv_sem, back_send_sem, back_recv_sem, wave_send, wave_recv,
    pair_send, pair_recv,
):
    me = lax.axis_index("wide")
    core = lax.axis_index("narrow")
    my_z, my_y, my_x = me % NZ, (me // NZ) % NY, me // (NZ * NY)
    first = waves[0]

    def push(src, dst, sem_out, sem_in, chip, on_core=core):
        return pltpu.make_async_remote_copy(
            src_ref=src, dst_ref=dst, send_sem=sem_out, recv_sem=sem_in,
            device_id=(chip, on_core), device_id_type=MESH,
        )

    loads = [
        pltpu.make_async_copy(spectra.at[pl.ds(0, UPPER)], spec_a, load_sem.at[0]),
        pltpu.make_async_copy(spectra.at[pl.ds(MIDDLE, SPAN)], spec_b, load_sem.at[1]),
    ]

    def chunk_of(step):
        return (my_x + step) % NX

    def load_leg(step, part):
        lanes = pl.ds(pl.multiple_of(chunk_of(step) * 128, 128), 128)
        span = pl.ds(0, UPPER) if part == 0 else pl.ds(UPPER, ROWS - UPPER)
        return pltpu.make_async_copy(
            legendre.at[span, lanes], leg.at[span, lanes], load_sem.at[2 + 2 * step + part]
        )

    loads[0].start()
    load_leg(0, 0).start()
    loads[1].start()
    load_leg(0, 1).start()
    for step in range(1, NX):
        load_leg(step, 0).start()
        load_leg(step, 1).start()

    barrier = pltpu.get_barrier_semaphore()

    def greet(i, carry):
        pl.semaphore_signal(
            barrier, inc=1, device_id=((me + i) % CHIPS, core), device_id_type=MESH
        )
        return carry

    lax.fori_loop(1, CHIPS, greet, 0)
    pl.semaphore_signal(barrier, inc=1, device_id=(me, 1 - core), device_id_type=MESH)

    block_z[...] = jnp.where(rows_iota((NZ, 128)) == my_z, first, 0)

    low_half = rows_iota((128, 128)) % 8 < 4

    def inverse(step):
        lanes = pl.ds(pl.multiple_of(chunk_of(step) * 128, 128), 128)
        if step == 0:
            loads[0].wait()
            middle = MIDDLE + rows_iota((UPPER - MIDDLE, 1))
            own = middle < UPPER - first
            here = spec_a[MIDDLE:UPPER, :]
            spec_a[MIDDLE:UPPER, :] = jnp.where(own, here, jnp.zeros_like(here))
        load_leg(step, 0).wait()
        wave_a = lax.dot_general(leg[0:UPPER, lanes], spec_a[...], ROW_ROW, preferred_element_type=F32)
        if step == 0:
            loads[1].wait()
            here = spec_b[0 : UPPER - MIDDLE, :]
            spec_b[0 : UPPER - MIDDLE, :] = jnp.where(own, jnp.zeros_like(here), here)
            here = spec_b[UPPER:SPAN, :]
            tail = MIDDLE + UPPER + rows_iota((SPAN - UPPER, 1)) < TOTAL
            spec_b[UPPER:SPAN, :] = jnp.where(tail, here, jnp.zeros_like(here))
        load_leg(step, 1).wait()
        wave_b = lax.dot_general(leg[MIDDLE:ROWS, lanes], spec_b[...], ROW_ROW, preferred_element_type=F32)
        even, odd = [], []
        for wave in (wave_a, wave_b):
            real, imag = wave[:, :128], wave[:, 128:]
            even.append(jnp.where(low_half, real, pltpu.roll(imag, 4, 0)).reshape(16, 8, 128))
            odd.append(jnp.where(low_half, pltpu.roll(real, 124, 0), imag).reshape(16, 8, 128))
        both = jnp.stack([jnp.concatenate(even, 1), jnp.concatenate(odd, 1)], axis=1)
        send[pl.ds(chunk_of(step) * 32, 32)] = both.reshape(32, 16, 128).astype(BF16)

    def push_chunk(step):
        def one(i, carry):
            chip = (chunk_of(step) * NY + (my_y + i // NZ) % NY) * NZ + (my_z + i) % NZ
            push(send.at[chip], recv.at[me], send_sem, recv_sem, chip).start()
            return carry

        lax.fori_loop(1 if step == 0 else 0, NY * NZ, one, 0)

    def z_push(d):
        chip = (my_x * NY + my_y) * NZ + (my_z + d) % NZ
        return push(block_z, from_z.at[d - 1], wave_send.at[0], wave_recv.at[0], chip)

    def y_push(d):
        chip = (my_x * NY + (my_y + d) % NY) * NZ + my_z
        return push(block_y, from_y.at[my_y], wave_send.at[1], wave_recv.at[1], chip)

    def x_push(d):
        chip = (((my_x + d) % NX) * NY + my_y) * NZ + my_z
        return push(block_x, from_x.at[my_x], wave_send.at[2], wave_recv.at[2], chip)

    inverse(0)
    pl.semaphore_wait(barrier, CHIPS)
    for d in range(1, NZ):
        z_push(d).start()
    push_chunk(0)
    recv[me] = send[me]
    inverse(1)
    push_chunk(1)
    pltpu.make_async_copy(from_z, from_z, wave_recv.at[0]).wait()
    block_y[...] = block_z[...] + jnp.sum(from_z[...], axis=0)
    from_y[my_y] = block_y[...]
    for d in range(1, NY):
        y_push(d).start()
    inverse(2)
    push_chunk(2)
    inverse(3)
    push_chunk(3)
    theirs = pl.ds(pl.multiple_of((1 - core) * MIDDLE, 32), SPAN)
    leg_push = push(leg.at[theirs], leg_x, pair_send.at[0], pair_recv.at[0], me, 1 - core)
    leg_push.start()
    pltpu.make_async_copy(from_y.at[pl.ds(0, NY - 1)], from_y.at[pl.ds(0, NY - 1)], wave_recv.at[1]).wait()
    block_x[...] = from_y[...].reshape(NY * NZ, 128)
    from_x[my_x] = block_x[...]
    for d in range(1, NX):
        x_push(d).start()

    harm[...] = jnp.zeros_like(harm)
    for l in range(4):
        for part in range(2):
            harm[pl.ds(2 * l + part, 1), 0 : BAND * 2 - 1] = coef[0, l, pl.ds(part, 1), :]
    for l in range(4):
        for part in range(2):
            line = jnp.broadcast_to(harm[pl.ds(2 * l + part, 1), :], (BAND, 2 * BAND))
            turned = pltpu.roll(line, BAND + 1, 1, stride=1, stride_axis=0)
            table[l, part] = turned[:, :BAND].astype(BF16)

    pltpu.make_async_copy(from_x.at[pl.ds(0, NX - 1)], from_x.at[pl.ds(0, NX - 1)], wave_recv.at[2]).wait()
    wave = from_x[...].reshape(CHIPS, 128)
    wave = jnp.concatenate([wave, wave], axis=1)
    falling = BAND - 1 - lax.broadcasted_iota(jnp.int32, (CHIPS, BAND), 1)
    picks = jnp.concatenate(
        [jnp.where(wave == falling, 1.0, 0.0), jnp.where(BAND - 1 - wave == falling, 1.0, 0.0)], axis=0
    ).astype(BF16)

    all_but_one = recv.at[pl.ds(0, CHIPS - 1)]
    pltpu.make_async_copy(all_but_one, all_but_one, recv_sem).wait()
    grid[...] = recv[...].astype(F32).reshape(CHIPS * 16, 128)
    columns = []
    for l in range(4):
        for part in range(2):
            columns.append(
                jnp.concatenate(
                    [grid[pl.ds(slot * 8 + part * 4 + l, CHIPS, stride=16), :] for slot in range(2)], axis=0
                )
            )
    by_slot = jnp.concatenate(columns, axis=1).astype(BF16)
    natural = lax.dot_general(picks, by_slot, ROW_ROW, preferred_element_type=F32)
    number = BAND - 1 - rows_iota((BAND, 1))
    scaled = []
    for l in range(4):
        resolved = number < lengths[0, l]
        here = natural[:, 256 * l : 256 * l + 256]
        masked = jnp.where(resolved, here, jnp.zeros_like(here)).astype(BF16)
        real = jnp.dot(table[l, 0], masked, preferred_element_type=F32)
        imag = jnp.dot(table[l, 1], masked, preferred_element_type=F32)
        coupled = jnp.concatenate(
            [real[:, :128] - imag[:, 128:], real[:, 128:] + imag[:, :128]], axis=1
        )
        coupled = coupled * weights[0, l]
        scaled.append(jnp.where(resolved, coupled, jnp.zeros_like(coupled)).astype(BF16))
    by_slot = jnp.dot(picks, jnp.concatenate(scaled, axis=1), preferred_element_type=F32)
    for l in range(4):
        for part in range(2):
            lanes = slice((2 * l + part) * 128, (2 * l + part) * 128 + 128)
            for slot in range(2):
                grid[pl.ds(slot * 8 + part * 4 + l, CHIPS, stride=16), :] = by_slot[
                    slot * CHIPS : slot * CHIPS + CHIPS, lanes
                ]
    send_back[...] = grid[...].reshape(CHIPS, 16, 128).astype(BF16)

    def push_back(i, carry):
        chip = (me + i) % CHIPS
        push(send_back.at[chip], recv_back.at[me], back_send_sem, back_recv_sem, chip).start()
        return carry

    lax.fori_loop(1, CHIPS, push_back, 0)
    recv_back[me] = send_back[me]

    all_back = recv_back.at[pl.ds(0, CHIPS - 1)]
    pltpu.make_async_copy(all_back, all_back, back_recv_sem).wait()
    arrived = recv_back[...].astype(F32).reshape(CHIPS // 2, 2, 16, 128)
    half = rows_iota((4 * CHIPS, 128)) % 8 < 4
    for slot in range(2):
        even = arrived[:, 0, 8 * slot : 8 * slot + 8].reshape(4 * CHIPS, 128)
        odd = arrived[:, 1, 8 * slot : 8 * slot + 8].reshape(4 * CHIPS, 128)
        real = jnp.where(half, even, pltpu.roll(odd, 4, 0))
        imag = jnp.where(half, pltpu.roll(even, 4 * CHIPS - 4, 0), odd)
        rows[slot] = jnp.concatenate([real, imag], axis=1).astype(BF16)
    rows_push = push(rows.at[1 - core], rows_x, pair_send.at[1], pair_recv.at[1], me, 1 - core)
    rows_push.start()
    base = core * MIDDLE
    for start in range(0, SPAN, BLOCK):
        size = min(BLOCK, SPAN - start)
        table_rows = leg[pl.ds(pl.multiple_of(base + start, 16), size), :]
        acc[start : start + size, :] = jnp.dot(table_rows, rows[core], preferred_element_type=F32)
    leg_push.wait_recv()
    rows_push.wait_recv()

    def finish(start, size):
        span = pl.ds(pl.multiple_of(start, 16), size)
        return acc[span, :] + jnp.dot(leg_x[span, :], rows_x[...], preferred_element_type=F32)

    mid[...] = finish((1 - core) * MIDDLE, 256).astype(BF16)
    mid_push = push(mid, mid_x, pair_send.at[2], pair_recv.at[2], me, 1 - core)
    mid_push.start()
    for i in range(MIDDLE // BLOCK):
        out[pl.ds(pl.multiple_of(core * 32 + i * BLOCK, 32), BLOCK), :] = finish(
            core * 256 + i * BLOCK, BLOCK
        ).astype(BF16)

    @pl.when(core == 1)
    def _():
        last = MIDDLE + UPPER + rows_iota((SPAN - UPPER, 1)) < TOTAL
        ending = finish(UPPER, SPAN - UPPER)
        ending = jnp.where(last, ending, jnp.zeros_like(ending)).astype(BF16)
        out[MIDDLE + 32 : MIDDLE + 48, :] = ending
        out[MIDDLE + 48 : SHARE, :] = jnp.zeros((SHARE - MIDDLE - 48, 256), BF16)

    mid_push.wait_recv()
    belongs = (MIDDLE + rows_iota((256, 1)) < UPPER - first).astype(jnp.int32)
    merged = jnp.where(belongs == 1 - core, mid[...], mid_x[...])

    @pl.when(core == 0)
    def _():
        out[MIDDLE:SHARE, :] = merged[: SHARE - MIDDLE]

    @pl.when(core == 1)
    def _():
        out[0:32, :] = merged[SHARE - MIDDLE :]

    for d in range(1, NZ):
        z_push(d).wait_send()
    for d in range(1, NY):
        y_push(d).wait_send()
    for d in range(1, NX):
        x_push(d).wait_send()
    pltpu.make_async_copy(all_but_one, all_but_one, send_sem).wait()
    pltpu.make_async_copy(all_back, all_back, back_send_sem).wait()
    leg_push.wait_send()
    rows_push.wait_send()
    mid_push.wait_send()


def shards(spectra, legendre, weights, coefficient, row_length, wave_number):
    message = pltpu.VMEM((CHIPS, 16, 128), BF16)
    vmem = pl.BlockSpec(memory_space=pltpu.VMEM)
    smem = pl.BlockSpec(memory_space=pltpu.SMEM)
    hbm = pl.BlockSpec(memory_space=pl.ANY)
    dma = pltpu.SemaphoreType.DMA
    return pl.pallas_call(
        kernel,
        out_shape=jax.ShapeDtypeStruct((SHARE, 256), BF16),
        in_specs=[hbm, hbm, smem, vmem, smem, smem],
        out_specs=vmem,
        scratch_shapes=[
            pltpu.VMEM((ROWS, 512), BF16),
            pltpu.VMEM((UPPER, 256), BF16),
            pltpu.VMEM((SPAN, 256), BF16),
            pltpu.VMEM((SPAN, 512), BF16),
            message, message, message, message,
            pltpu.VMEM((CHIPS * 16, 128), F32),
            pltpu.VMEM((8, 2 * BAND), F32),
            pltpu.VMEM((4, 2, BAND, BAND), BF16),
            pltpu.VMEM((NZ, 128), jnp.int32),
            pltpu.VMEM((NZ - 1, NZ, 128), jnp.int32),
            pltpu.VMEM((NZ, 128), jnp.int32),
            pltpu.VMEM((NY, NZ, 128), jnp.int32),
            pltpu.VMEM((NY * NZ, 128), jnp.int32),
            pltpu.VMEM((NX, NY * NZ, 128), jnp.int32),
            pltpu.VMEM((2, 512, 256), BF16),
            pltpu.VMEM((512, 256), BF16),
            pltpu.VMEM((SPAN, 256), F32),
            pltpu.VMEM((256, 256), BF16),
            pltpu.VMEM((256, 256), BF16),
            dma((2 + 2 * NX,)), dma, dma, dma, dma, dma((3,)), dma((3,)), dma((3,)), dma((3,)),
        ],
        compiler_params=pltpu.CompilerParams(
            collective_id=0, has_side_effects=True, vmem_limit_bytes=56 * 1024 * 1024
        ),
        name="transforms",
    )(spectra, legendre, weights, coefficient, row_length, wave_number)


def solution(mesh):
    return jax.shard_map(
        shards,
        mesh=mesh,
        in_specs=(
            P("wide", None),
            P("wide", "narrow"),
            P("narrow", "wide"),
            P("narrow", "wide", None, None),
            P("narrow", "wide"),
            P("wide"),
        ),
        out_specs=P(("wide", "narrow"), None),
        check_vma=False,
    )
```

```python
import functools

import jax
import jax.numpy as jnp
from jax import lax
from jax.experimental import pallas as pl
from jax.experimental.pallas import tpu as pltpu
from jax.sharding import PartitionSpec as P

TRUNC = 3999
NX, NY, NZ = 4, 4, 8
CHIPS = NX * NY * NZ
BAND = 2 * CHIPS
MIDDLE = 3744
UPPER = TRUNC + 1
TOTAL = 2 * TRUNC + 3 - BAND
SPAN = 4016
ROWS = MIDDLE + SPAN
SHARE = 3968
BLOCK = 416
MESH = pl.DeviceIdType.MESH
BF16, F32 = jnp.bfloat16, jnp.float32
ROW_ROW = (((0,), (0,)), ((), ()))


def rows_iota(shape):
    return lax.broadcasted_iota(jnp.int32, shape, 0)


def swap_blocks(a, b, c, d, sizes):
    place = rows_iota(a.shape) % 8
    n = a.shape[0]
    for size in sizes:
        keep = place % (2 * size) < size

        def trade(p, q):
            return jnp.where(keep, p, pltpu.roll(q, size, 0)), jnp.where(keep, pltpu.roll(p, n - size, 0), q)

        if size == 4:
            a, c = trade(a, c)
            b, d = trade(b, d)
        else:
            a, b = trade(a, b)
            c, d = trade(c, d)
    return a, b, c, d


def couple_kernel(
    spectra, legendre, weights_in, coef_in, lengths_in, waves_in, acc, acc_mid, leg_x, rows_x,
    weights, coef, lengths, waves, leg, spec_a, spec_b, send, recv, send_back, recv_back, from_pair, grid, harm, table,
    block_z, from_z, block_y, from_y, block_x, from_x, rows,
    load_sem, small_sem, send_sem, recv_sem, back_send_sem, back_recv_sem, wave_send, wave_recv,
    pair_send, pair_recv,
):
    me = lax.axis_index("wide")
    core = lax.axis_index("narrow")
    my_z, my_y, my_x = me % NZ, (me // NZ) % NY, me // (NZ * NY)

    def push(src, dst, sem_out, sem_in, chip, on_core=core):
        return pltpu.make_async_remote_copy(
            src_ref=src, dst_ref=dst, send_sem=sem_out, recv_sem=sem_in,
            device_id=(chip, on_core), device_id_type=MESH,
        )

    small = [
        pltpu.make_async_copy(src, dst, small_sem.at[i])
        for i, (src, dst) in enumerate(
            [(waves_in, waves), (lengths_in, lengths), (weights_in, weights), (coef_in, coef)]
        )
    ]
    loads = [
        pltpu.make_async_copy(spectra.at[pl.ds(0, UPPER)], spec_a, load_sem.at[0]),
        pltpu.make_async_copy(spectra.at[pl.ds(MIDDLE, SPAN)], spec_b, load_sem.at[1]),
    ]

    def chunk_of(step):
        return (my_x + step) % NX

    def load_leg(step, part):
        lanes = pl.ds(pl.multiple_of(chunk_of(step) * 128, 128), 128)
        span = pl.ds(0, UPPER) if part == 0 else pl.ds(UPPER, ROWS - UPPER)
        return pltpu.make_async_copy(
            legendre.at[span, lanes], leg.at[span, lanes], load_sem.at[2 + 2 * step + part]
        )

    small[0].start()
    loads[0].start()
    load_leg(0, 0).start()
    loads[1].start()
    load_leg(0, 1).start()
    for copy in small[1:]:
        copy.start()

    barrier = pltpu.get_barrier_semaphore()

    def greet(i, carry):
        pl.semaphore_signal(
            barrier, inc=1, device_id=(lax.rem(me + i, CHIPS), core), device_id_type=MESH
        )
        return carry

    lax.fori_loop(1, CHIPS, greet, 0, unroll=8)
    pl.semaphore_signal(barrier, inc=1, device_id=(me, 1 - core), device_id_type=MESH)

    small[0].wait()
    first = waves[0]
    block_z[...] = jnp.where(rows_iota((NZ, 128)) == my_z, first, 0)

    def inverse(step):
        lanes = pl.ds(pl.multiple_of(chunk_of(step) * 128, 128), 128)
        if step == 0:
            loads[0].wait()
            load_leg(1, 0).start()
            middle = MIDDLE + rows_iota((UPPER - MIDDLE, 1))
            own = middle < UPPER - first
            here = spec_a[MIDDLE:UPPER, :]
            spec_a[MIDDLE:UPPER, :] = jnp.where(own, here, jnp.zeros_like(here))
        load_leg(step, 0).wait()
        if step == 0:
            load_leg(1, 1).start()
        elif step < 3:
            load_leg(step + 1, 1).start()
        wave_a = lax.dot_general(leg[0:UPPER, lanes], spec_a[...], ROW_ROW, preferred_element_type=F32)
        if step == 0:
            loads[1].wait()
            load_leg(2, 0).start()
            here = spec_b[0 : UPPER - MIDDLE, :]
            spec_b[0 : UPPER - MIDDLE, :] = jnp.where(own, jnp.zeros_like(here), here)
            here = spec_b[UPPER:SPAN, :]
            tail = MIDDLE + UPPER + rows_iota((SPAN - UPPER, 1)) < TOTAL
            spec_b[UPPER:SPAN, :] = jnp.where(tail, here, jnp.zeros_like(here))
        load_leg(step, 1).wait()
        if step == 1:
            load_leg(3, 0).start()
        wave_b = lax.dot_general(leg[MIDDLE:ROWS, lanes], spec_b[...], ROW_ROW, preferred_element_type=F32)
        even0, even1, odd0, odd1 = swap_blocks(
            wave_a[:, :128], wave_a[:, 128:], wave_b[:, :128], wave_b[:, 128:], (4, 2)
        )
        for c, (even, odd) in enumerate(((even0, odd0), (even1, odd1))):
            both = jnp.stack([even.reshape(16, 8, 128), odd.reshape(16, 8, 128)], axis=1)
            send[c, pl.ds(chunk_of(step) * 32, 32)] = both.reshape(32, 8, 128).astype(BF16)

    def push_chunk(c, step):
        for dy in range(NY):
            line = (chunk_of(step) * NY + lax.rem(my_y + dy, NY)) * NZ

            def one(i, carry):
                chip = line + lax.rem(my_z + i, NZ)
                push(send.at[c, chip], recv.at[c, me], send_sem.at[c], recv_sem.at[c], chip).start()
                return carry

            lax.fori_loop(1 if step == 0 and dy == 0 else 0, NZ, one, 0, unroll=4)

    def z_push(d):
        chip = (my_x * NY + my_y) * NZ + (my_z + d) % NZ
        return push(block_z, from_z.at[d - 1], wave_send.at[0], wave_recv.at[0], chip)

    def y_push(d):
        chip = (my_x * NY + (my_y + d) % NY) * NZ + my_z
        return push(block_y, from_y.at[my_y], wave_send.at[1], wave_recv.at[1], chip)

    def x_push(d):
        chip = (((my_x + d) % NX) * NY + my_y) * NZ + my_z
        return push(block_x, from_x.at[my_x], wave_send.at[2], wave_recv.at[2], chip)

    inverse(0)
    inverse(1)
    pl.semaphore_wait(barrier, CHIPS)
    for d in range(1, NZ):
        z_push(d).start()
    push_chunk(0, 0)
    push_chunk(0, 1)
    inverse(2)
    push_chunk(0, 2)
    inverse(3)
    push_chunk(0, 3)
    pltpu.make_async_copy(from_z, from_z, wave_recv.at[0]).wait()
    block_y[...] = block_z[...] + jnp.sum(from_z[...], axis=0)
    from_y[my_y] = block_y[...]
    for d in range(1, NY):
        y_push(d).start()
    for step in range(NX):
        push_chunk(1, step)
    for c in range(2):
        recv[c, me] = send[c, me]
    pltpu.make_async_copy(from_y.at[pl.ds(0, NY - 1)], from_y.at[pl.ds(0, NY - 1)], wave_recv.at[1]).wait()
    block_x[...] = from_y[...].reshape(NY * NZ, 128)
    from_x[my_x] = block_x[...]
    for d in range(1, NX):
        x_push(d).start()

    for copy in small[1:]:
        copy.wait()
    harm[...] = jnp.zeros_like(harm)
    for l in range(4):
        for part in range(2):
            harm[pl.ds(2 * l + part, 1), 0 : BAND * 2 - 1] = coef[0, l, pl.ds(part, 1), :]
    for l in range(4):
        for part in range(2):
            line = jnp.broadcast_to(harm[pl.ds(2 * l + part, 1), :], (BAND, 2 * BAND))
            turned = pltpu.roll(line, BAND + 1, 1, stride=1, stride_axis=0)
            table[l, part] = turned[:, :BAND].astype(BF16)

    pltpu.make_async_copy(from_x.at[pl.ds(0, NX - 1)], from_x.at[pl.ds(0, NX - 1)], wave_recv.at[2]).wait()
    wave = from_x[...].reshape(CHIPS, 128)
    wave = jnp.concatenate([wave, wave], axis=1)
    falling = BAND - 1 - lax.broadcasted_iota(jnp.int32, (CHIPS, BAND), 1)
    picks = jnp.concatenate(
        [jnp.where(wave == falling, 1.0, 0.0), jnp.where(BAND - 1 - wave == falling, 1.0, 0.0)], axis=0
    ).astype(BF16)
    number = BAND - 1 - rows_iota((BAND, 1))

    def arrival(buffer, c, sem):
        part = buffer.at[c, pl.ds(0, CHIPS - 1)]
        return pltpu.make_async_copy(part, part, sem.at[c])

    def couple(c):
        arrival(recv, c, recv_sem).wait()
        grid[...] = recv[c].astype(F32).reshape(CHIPS * 8, 128)
        columns = []
        for l in range(2):
            for part in range(2):
                columns.append(
                    jnp.concatenate(
                        [grid[pl.ds(slot * 4 + part * 2 + l, CHIPS, stride=8), :] for slot in range(2)], axis=0
                    )
                )
        by_slot = jnp.concatenate(columns, axis=1).astype(BF16)
        natural = lax.dot_general(picks, by_slot, ROW_ROW, preferred_element_type=F32)
        scaled = []
        for l in range(2):
            row = 2 * c + l
            resolved = number < lengths[0, row]
            here = natural[:, 256 * l : 256 * l + 256]
            masked = jnp.where(resolved, here, jnp.zeros_like(here)).astype(BF16)
            real = jnp.dot(table[row, 0], masked, preferred_element_type=F32)
            imag = jnp.dot(table[row, 1], masked, preferred_element_type=F32)
            coupled = jnp.concatenate(
                [real[:, :128] - imag[:, 128:], real[:, 128:] + imag[:, :128]], axis=1
            )
            coupled = coupled * weights[0, row]
            scaled.append(jnp.where(resolved, coupled, jnp.zeros_like(coupled)).astype(BF16))
        by_slot = jnp.dot(picks, jnp.concatenate(scaled, axis=1), preferred_element_type=F32)
        for l in range(2):
            for part in range(2):
                lanes = slice((2 * l + part) * 128, (2 * l + part) * 128 + 128)
                for slot in range(2):
                    grid[pl.ds(slot * 4 + part * 2 + l, CHIPS, stride=8), :] = by_slot[
                        slot * CHIPS : slot * CHIPS + CHIPS, lanes
                    ]
        send_back[c] = grid[...].reshape(CHIPS, 8, 128).astype(BF16)

        def push_back(i, carry):
            chip = lax.rem(me + i, CHIPS)
            push(
                send_back.at[c, chip], recv_back.at[c, me], back_send_sem.at[c], back_recv_sem.at[c], chip
            ).start()
            return carry

        lax.fori_loop(1, CHIPS, push_back, 0, unroll=4)
        recv_back[c, me] = send_back[c, me]

    couple(0)
    couple(1)
    theirs = pl.ds(pl.multiple_of((1 - core) * MIDDLE, 32), SPAN)
    leg_push = push(leg.at[theirs], leg_x, pair_send.at[0], pair_recv.at[0], me, 1 - core)
    leg_push.start()

    def swap(c):
        return push(recv_back.at[c], from_pair.at[c], pair_send.at[1 + c], pair_recv.at[1 + c], me, 1 - core)

    def by_latitude(buffer, target):
        arrived = []
        for c in range(2):
            parts = buffer[c].astype(F32).reshape(CHIPS // 2, 2, 8, 128)
            arrived.append((parts[:, 0].reshape(4 * CHIPS, 128), parts[:, 1].reshape(4 * CHIPS, 128)))
        (even0, odd0), (even1, odd1) = arrived
        real_a, imag_a, real_b, imag_b = swap_blocks(even0, even1, odd0, odd1, (2, 4))
        target[0] = jnp.concatenate([real_a, imag_a], axis=1).astype(BF16)
        target[1] = jnp.concatenate([real_b, imag_b], axis=1).astype(BF16)

    for c in range(2):
        arrival(recv_back, c, back_recv_sem).wait()
        swap(c).start()
    by_latitude(recv_back, rows)
    base = core * MIDDLE
    acc_mid[...] = jnp.dot(leg[MIDDLE:UPPER, :], rows[1 - core], preferred_element_type=F32)
    for start in range(0, SPAN, BLOCK):
        size = min(BLOCK, SPAN - start)
        table_rows = leg[pl.ds(pl.multiple_of(base + start, 16), size), :]
        acc[start : start + size, :] = jnp.dot(table_rows, rows[core], preferred_element_type=F32)

    for d in range(1, NZ):
        z_push(d).wait_send()
    for d in range(1, NY):
        y_push(d).wait_send()
    for d in range(1, NX):
        x_push(d).wait_send()
    for c in range(2):
        arrival(recv, c, send_sem).wait()
        arrival(recv_back, c, back_send_sem).wait()
    leg_push.wait()
    for c in range(2):
        swap(c).wait()
    by_latitude(from_pair, rows_x)


def finish_kernel(waves, acc, acc_mid, leg_x, rows_x, out, ready, sem):
    core = lax.axis_index("narrow")
    copies = []

    def place(start, size, value, i):
        span = pl.ds(pl.multiple_of(start, 16), size)
        ready[span, :] = value
        copy = pltpu.make_async_copy(ready.at[span], out.at[span], sem.at[i])
        copy.start()
        return copy

    def finish(start, size):
        span = pl.ds(pl.multiple_of(start, 16), size)
        return acc[span, :] + jnp.dot(leg_x[span, :], rows_x[core], preferred_element_type=F32)

    middle = pl.ds(pl.multiple_of((1 - core) * MIDDLE, 32), 256)
    mine = finish((1 - core) * MIDDLE, 256)
    other = acc_mid[...] + jnp.dot(leg_x[middle, :], rows_x[1 - core], preferred_element_type=F32)
    in_first = (MIDDLE + rows_iota((256, 1)) < UPPER - waves[0]).astype(jnp.int32)
    merged = jnp.where(in_first == 1 - core, mine, other).astype(BF16)

    @pl.when(core == 0)
    def _():
        place(MIDDLE, SHARE - MIDDLE, merged[: SHARE - MIDDLE], 0)

    @pl.when(core == 1)
    def _():
        last = MIDDLE + UPPER + rows_iota((SPAN - UPPER, 1)) < TOTAL
        ending = finish(UPPER, SPAN - UPPER)
        ready[MIDDLE + 32 : MIDDLE + 48, :] = jnp.where(last, ending, jnp.zeros_like(ending)).astype(BF16)
        ready[MIDDLE + 48 : SHARE, :] = jnp.zeros((SHARE - MIDDLE - 48, 256), BF16)
        ready[0:32, :] = merged[SHARE - MIDDLE :]
        pltpu.make_async_copy(ready.at[0:32], out.at[0:32], sem.at[0]).start()
        pltpu.make_async_copy(ready.at[MIDDLE + 32 : SHARE], out.at[MIDDLE + 32 : SHARE], sem.at[0]).start()

    for i in range(MIDDLE // BLOCK):
        value = finish(core * 256 + i * BLOCK, BLOCK).astype(BF16)
        copies.append(place(core * 32 + i * BLOCK, BLOCK, value, 1 + i))
    for copy in copies:
        copy.wait()
    pltpu.make_async_copy(ready.at[MIDDLE:SHARE], out.at[MIDDLE:SHARE], sem.at[0]).wait()


def shards(spectra, legendre, weights, coefficient, row_length, wave_number):
    message = pltpu.VMEM((2, CHIPS, 8, 128), BF16)
    vmem = pl.BlockSpec(memory_space=pltpu.VMEM)
    smem = pl.BlockSpec(memory_space=pltpu.SMEM)
    hbm = pl.BlockSpec(memory_space=pltpu.HBM)
    dma = pltpu.SemaphoreType.DMA
    acc, acc_mid, leg_x, rows_x = pl.pallas_call(
        couple_kernel,
        out_shape=[
            pltpu.VMEM((SPAN, 256), F32),
            pltpu.VMEM((256, 256), F32),
            pltpu.VMEM((SPAN, 512), BF16),
            pltpu.VMEM((2, 512, 256), BF16),
        ],
        in_specs=[hbm] * 6,
        out_specs=[vmem] * 4,
        scratch_shapes=[
            pltpu.SMEM((1, 4), F32),
            pltpu.VMEM((1, 4, 2, 2 * BAND - 1), F32),
            pltpu.SMEM((1, 4), jnp.int32),
            pltpu.SMEM((2,), jnp.int32),
            pltpu.VMEM((ROWS, 512), BF16),
            pltpu.VMEM((UPPER, 256), BF16),
            pltpu.VMEM((SPAN, 256), BF16),
            message, message, message, message, message,
            pltpu.VMEM((CHIPS * 8, 128), F32),
            pltpu.VMEM((8, 2 * BAND), F32),
            pltpu.VMEM((4, 2, BAND, BAND), BF16),
            pltpu.VMEM((NZ, 128), jnp.int32),
            pltpu.VMEM((NZ - 1, NZ, 128), jnp.int32),
            pltpu.VMEM((NZ, 128), jnp.int32),
            pltpu.VMEM((NY, NZ, 128), jnp.int32),
            pltpu.VMEM((NY * NZ, 128), jnp.int32),
            pltpu.VMEM((NX, NY * NZ, 128), jnp.int32),
            pltpu.VMEM((2, 512, 256), BF16),
            dma((2 + 2 * NX,)), dma((4,)), dma((2,)), dma((2,)), dma((2,)), dma((2,)),
            dma((3,)), dma((3,)), dma((3,)), dma((3,)),
        ],
        compiler_params=pltpu.CompilerParams(
            collective_id=0, has_side_effects=True, vmem_limit_bytes=48 * 1024 * 1024
        ),
        name="transforms",
    )(spectra, legendre, weights, coefficient, row_length, wave_number)
    return pl.pallas_call(
        finish_kernel,
        out_shape=jax.ShapeDtypeStruct((SHARE, 256), BF16),
        in_specs=[smem, vmem, vmem, vmem, vmem],
        out_specs=hbm,
        scratch_shapes=[pltpu.VMEM((SHARE, 256), BF16), dma((1 + MIDDLE // BLOCK,))],
        compiler_params=pltpu.CompilerParams(vmem_limit_bytes=48 * 1024 * 1024),
        name="finish",
    )(wave_number, *[pltpu.with_memory_space_constraint(a, pltpu.VMEM) for a in (acc, acc_mid, leg_x, rows_x)])


def solution(mesh):
    return jax.shard_map(
        shards,
        mesh=mesh,
        in_specs=(
            P("wide", None),
            P("wide", "narrow"),
            P("narrow", "wide"),
            P("narrow", "wide", None, None),
            P("narrow", "wide"),
            P("wide"),
        ),
        out_specs=P(("wide", "narrow"), None),
        check_vma=False,
    )
```

```python
import functools

import jax
import jax.numpy as jnp
from jax import lax
from jax.experimental import pallas as pl
from jax.experimental.pallas import tpu as pltpu
from jax.sharding import PartitionSpec as P

TRUNC = 3999
NX, NY, NZ = 4, 4, 8
CHIPS = NX * NY * NZ
BAND = 2 * CHIPS
MIDDLE = 3744
UPPER = TRUNC + 1
TOTAL = 2 * TRUNC + 3 - BAND
SPAN = 4016
ROWS = MIDDLE + SPAN
SHARE = 3968
BLOCK = 416
Z_ORDER = (0, 3, 1, 2, 4, 7, 5, 6)
MESH = pl.DeviceIdType.MESH
BF16, F32 = jnp.bfloat16, jnp.float32
ROW_ROW = (((0,), (0,)), ((), ()))


def rows_iota(shape):
    return lax.broadcasted_iota(jnp.int32, shape, 0)


def swap_blocks(a, b, c, d, sizes):
    place = rows_iota(a.shape) % 8
    n = a.shape[0]
    for size in sizes:
        keep = place % (2 * size) < size

        def trade(p, q):
            return jnp.where(keep, p, pltpu.roll(q, size, 0)), jnp.where(keep, pltpu.roll(p, n - size, 0), q)

        if size == 4:
            a, c = trade(a, c)
            b, d = trade(b, d)
        else:
            a, b = trade(a, b)
            c, d = trade(c, d)
    return a, b, c, d


def couple_kernel(
    spectra, legendre, weights_in, coef_in, lengths_in, waves_in, acc, acc_mid, leg_x, rows_x, own_mid,
    weights, coef, lengths, waves, leg, spec_a, spec_b, send, recv, send_back, recv_back, from_pair, grid, harm, table,
    block_z, from_z, block_y, from_y, block_x, from_x, rows,
    load_sem, small_sem, send_sem, recv_sem, back_send_sem, back_recv_sem, wave_send, wave_recv,
    pair_send, pair_recv,
):
    me = lax.axis_index("wide")
    core = lax.axis_index("narrow")
    my_z, my_y, my_x = me % NZ, (me // NZ) % NY, me // (NZ * NY)

    def push(src, dst, sem_out, sem_in, chip, on_core=core):
        return pltpu.make_async_remote_copy(
            src_ref=src, dst_ref=dst, send_sem=sem_out, recv_sem=sem_in,
            device_id=(chip, on_core), device_id_type=MESH,
        )

    small = [
        pltpu.make_async_copy(src, dst, small_sem.at[i])
        for i, (src, dst) in enumerate(
            [(waves_in, waves), (lengths_in, lengths), (weights_in, weights), (coef_in, coef)]
        )
    ]
    loads = [
        pltpu.make_async_copy(spectra.at[pl.ds(0, UPPER)], spec_a, load_sem.at[0]),
        pltpu.make_async_copy(spectra.at[pl.ds(MIDDLE, SPAN)], spec_b, load_sem.at[1]),
    ]

    def chunk_of(step):
        return (my_x + step) % NX

    def load_leg(step, part):
        lanes = pl.ds(pl.multiple_of(chunk_of(step) * 128, 128), 128)
        span = pl.ds(0, UPPER) if part == 0 else pl.ds(UPPER, ROWS - UPPER)
        return pltpu.make_async_copy(
            legendre.at[span, lanes], leg.at[span, lanes], load_sem.at[2 + 2 * step + part]
        )

    small[0].start()
    loads[0].start()
    load_leg(0, 0).start()
    loads[1].start()
    load_leg(0, 1).start()
    for copy in small[1:]:
        copy.start()

    barrier = pltpu.get_barrier_semaphore()

    def greet(i, carry):
        pl.semaphore_signal(
            barrier, inc=1, device_id=(lax.rem(me + i, CHIPS), core), device_id_type=MESH
        )
        return carry

    lax.fori_loop(1, CHIPS, greet, 0, unroll=8)
    pl.semaphore_signal(barrier, inc=1, device_id=(me, 1 - core), device_id_type=MESH)

    small[0].wait()
    first = waves[0]
    in_first = (MIDDLE + rows_iota((256, 256)) < UPPER - first).astype(jnp.int32)
    own_mid[...] = jnp.where(in_first == 1 - core, 1, 0)
    block_z[...] = jnp.where(rows_iota((NZ, 128)) == my_z, first, 0)

    def inverse(step):
        lanes = pl.ds(pl.multiple_of(chunk_of(step) * 128, 128), 128)
        if step == 0:
            loads[0].wait()
            load_leg(1, 0).start()
            middle = MIDDLE + rows_iota((UPPER - MIDDLE, 1))
            own = middle < UPPER - first
            here = spec_a[MIDDLE:UPPER, :]
            spec_a[MIDDLE:UPPER, :] = jnp.where(own, here, jnp.zeros_like(here))
        load_leg(step, 0).wait()
        if step == 0:
            load_leg(1, 1).start()
        elif step < 3:
            load_leg(step + 1, 1).start()
        wave_a = lax.dot_general(leg[0:UPPER, lanes], spec_a[...], ROW_ROW, preferred_element_type=F32)
        if step == 0:
            loads[1].wait()
            load_leg(2, 0).start()
            here = spec_b[0 : UPPER - MIDDLE, :]
            spec_b[0 : UPPER - MIDDLE, :] = jnp.where(own, jnp.zeros_like(here), here)
            here = spec_b[UPPER:SPAN, :]
            tail = MIDDLE + UPPER + rows_iota((SPAN - UPPER, 1)) < TOTAL
            spec_b[UPPER:SPAN, :] = jnp.where(tail, here, jnp.zeros_like(here))
        load_leg(step, 1).wait()
        if step == 1:
            load_leg(3, 0).start()
        wave_b = lax.dot_general(leg[MIDDLE:ROWS, lanes], spec_b[...], ROW_ROW, preferred_element_type=F32)
        even0, even1, odd0, odd1 = swap_blocks(
            wave_a[:, :128], wave_a[:, 128:], wave_b[:, :128], wave_b[:, 128:], (4, 2)
        )
        for c, (even, odd) in enumerate(((even0, odd0), (even1, odd1))):
            both = jnp.stack([even.reshape(16, 8, 128), odd.reshape(16, 8, 128)], axis=1)
            send[c, pl.ds(chunk_of(step) * 32, 32)] = both.reshape(32, 8, 128).astype(BF16)

    def push_chunk(c, step):
        for dy in range(NY):
            line = (chunk_of(step) * NY + lax.rem(my_y + dy, NY)) * NZ

            def one(i, carry):
                chip = line + lax.rem(my_z + i, NZ)
                push(send.at[c, chip], recv.at[c, me], send_sem.at[c], recv_sem.at[c], chip).start()
                return carry

            lax.fori_loop(1 if step == 0 and dy == 0 else 0, NZ, one, 0, unroll=4)

    def z_push(d):
        chip = (my_x * NY + my_y) * NZ + (my_z + d) % NZ
        return push(block_z, from_z.at[d - 1], wave_send.at[0], wave_recv.at[0], chip)

    def y_push(d):
        chip = (my_x * NY + (my_y + d) % NY) * NZ + my_z
        return push(block_y, from_y.at[my_y], wave_send.at[1], wave_recv.at[1], chip)

    def x_push(d):
        chip = (((my_x + d) % NX) * NY + my_y) * NZ + my_z
        return push(block_x, from_x.at[my_x], wave_send.at[2], wave_recv.at[2], chip)

    inverse(0)
    pl.semaphore_wait(barrier, CHIPS)
    for d in range(1, NZ):
        z_push(d).start()
    push_chunk(0, 0)
    inverse(1)
    push_chunk(0, 1)
    inverse(2)
    push_chunk(0, 2)
    inverse(3)
    push_chunk(0, 3)
    pltpu.make_async_copy(from_z, from_z, wave_recv.at[0]).wait()
    block_y[...] = block_z[...] + jnp.sum(from_z[...], axis=0)
    from_y[my_y] = block_y[...]
    for d in range(1, NY):
        y_push(d).start()
    for step in range(NX):
        push_chunk(1, step)
    for c in range(2):
        recv[c, me] = send[c, me]
    pltpu.make_async_copy(from_y.at[pl.ds(0, NY - 1)], from_y.at[pl.ds(0, NY - 1)], wave_recv.at[1]).wait()
    block_x[...] = from_y[...].reshape(NY * NZ, 128)
    from_x[my_x] = block_x[...]
    for d in range(1, NX):
        x_push(d).start()

    for copy in small[1:]:
        copy.wait()
    harm[...] = jnp.zeros_like(harm)
    for l in range(4):
        for part in range(2):
            harm[pl.ds(2 * l + part, 1), 0 : BAND * 2 - 1] = coef[0, l, pl.ds(part, 1), :]
    for l in range(4):
        for part in range(2):
            line = jnp.broadcast_to(harm[pl.ds(2 * l + part, 1), :], (BAND, 2 * BAND))
            turned = pltpu.roll(line, BAND + 1, 1, stride=1, stride_axis=0)
            table[l, part] = turned[:, :BAND].astype(BF16)

    pltpu.make_async_copy(from_x.at[pl.ds(0, NX - 1)], from_x.at[pl.ds(0, NX - 1)], wave_recv.at[2]).wait()
    wave = from_x[...].reshape(CHIPS, 128)
    wave = jnp.concatenate([wave, wave], axis=1)
    falling = BAND - 1 - lax.broadcasted_iota(jnp.int32, (CHIPS, BAND), 1)
    picks = jnp.concatenate(
        [jnp.where(wave == falling, 1.0, 0.0), jnp.where(BAND - 1 - wave == falling, 1.0, 0.0)], axis=0
    ).astype(BF16)
    number = BAND - 1 - rows_iota((BAND, 1))

    def arrival(buffer, c, sem):
        part = buffer.at[c, pl.ds(0, CHIPS - 1)]
        return pltpu.make_async_copy(part, part, sem.at[c])

    def couple(c):
        arrival(recv, c, recv_sem).wait()
        grid[...] = recv[c].astype(F32).reshape(CHIPS * 8, 128)
        columns = []
        for l in range(2):
            for part in range(2):
                columns.append(
                    jnp.concatenate(
                        [grid[pl.ds(slot * 4 + part * 2 + l, CHIPS, stride=8), :] for slot in range(2)], axis=0
                    )
                )
        by_slot = jnp.concatenate(columns, axis=1).astype(BF16)
        natural = lax.dot_general(picks, by_slot, ROW_ROW, preferred_element_type=F32)
        scaled = []
        for l in range(2):
            row = 2 * c + l
            resolved = number < lengths[0, row]
            here = natural[:, 256 * l : 256 * l + 256]
            masked = jnp.where(resolved, here, jnp.zeros_like(here)).astype(BF16)
            real = jnp.dot(table[row, 0], masked, preferred_element_type=F32)
            imag = jnp.dot(table[row, 1], masked, preferred_element_type=F32)
            coupled = jnp.concatenate(
                [real[:, :128] - imag[:, 128:], real[:, 128:] + imag[:, :128]], axis=1
            )
            coupled = coupled * weights[0, row]
            scaled.append(jnp.where(resolved, coupled, jnp.zeros_like(coupled)).astype(BF16))
        by_slot = jnp.dot(picks, jnp.concatenate(scaled, axis=1), preferred_element_type=F32)
        for l in range(2):
            for part in range(2):
                lanes = slice((2 * l + part) * 128, (2 * l + part) * 128 + 128)
                for slot in range(2):
                    grid[pl.ds(slot * 4 + part * 2 + l, CHIPS, stride=8), :] = by_slot[
                        slot * CHIPS : slot * CHIPS + CHIPS, lanes
                    ]
        send_back[c] = grid[...].reshape(CHIPS, 8, 128).astype(BF16)

        def push_back(chip):
            push(
                send_back.at[c, chip], recv_back.at[c, me], back_send_sem.at[c], back_recv_sem.at[c], chip
            ).start()

        for z in Z_ORDER:

            def one(i, carry):
                push_back((lax.rem(my_x + i // NY, NX) * NY + lax.rem(my_y + i, NY)) * NZ + z)
                return carry

            lax.fori_loop(1, NX * NY, one, 0, unroll=5)

            @pl.when(my_z != z)
            def _():
                push_back((my_x * NY + my_y) * NZ + z)

        recv_back[c, me] = send_back[c, me]

    couple(0)
    couple(1)
    theirs = pl.ds(pl.multiple_of((1 - core) * MIDDLE, 32), SPAN)
    leg_push = push(leg.at[theirs], leg_x, pair_send.at[0], pair_recv.at[0], me, 1 - core)
    leg_push.start()

    def swap(c):
        return push(recv_back.at[c], from_pair.at[c], pair_send.at[1 + c], pair_recv.at[1 + c], me, 1 - core)

    def by_latitude(buffer, target):
        arrived = []
        for c in range(2):
            parts = buffer[c].astype(F32).reshape(CHIPS // 2, 2, 8, 128)
            arrived.append((parts[:, 0].reshape(4 * CHIPS, 128), parts[:, 1].reshape(4 * CHIPS, 128)))
        (even0, odd0), (even1, odd1) = arrived
        real_a, imag_a, real_b, imag_b = swap_blocks(even0, even1, odd0, odd1, (2, 4))
        target[0] = jnp.concatenate([real_a, imag_a], axis=1).astype(BF16)
        target[1] = jnp.concatenate([real_b, imag_b], axis=1).astype(BF16)

    for c in range(2):
        arrival(recv_back, c, back_recv_sem).wait()
        swap(c).start()
    by_latitude(recv_back, rows)
    base = core * MIDDLE
    acc_mid[...] = jnp.dot(leg[MIDDLE:UPPER, :], rows[1 - core], preferred_element_type=F32)
    for start in range(0, SPAN, BLOCK):
        size = min(BLOCK, SPAN - start)
        table_rows = leg[pl.ds(pl.multiple_of(base + start, 16), size), :]
        acc[start : start + size, :] = jnp.dot(table_rows, rows[core], preferred_element_type=F32)

    for d in range(1, NZ):
        z_push(d).wait_send()
    for d in range(1, NY):
        y_push(d).wait_send()
    for d in range(1, NX):
        x_push(d).wait_send()
    for c in range(2):
        arrival(recv, c, send_sem).wait()
        arrival(recv_back, c, back_send_sem).wait()
    leg_push.wait()
    for c in range(2):
        swap(c).wait()
    by_latitude(from_pair, rows_x)


def finish_kernel(acc, acc_mid, leg_x, rows_x, own_mid, out, ready, sem):
    core = lax.axis_index("narrow")
    copies = []

    def place(start, size, value, i):
        span = pl.ds(pl.multiple_of(start, 16), size)
        ready[span, :] = value
        copy = pltpu.make_async_copy(ready.at[span], out.at[span], sem.at[i])
        copy.start()
        return copy

    def finish(start, size):
        span = pl.ds(pl.multiple_of(start, 16), size)
        return acc[span, :] + jnp.dot(leg_x[span, :], rows_x[core], preferred_element_type=F32)

    middle = pl.ds(pl.multiple_of((1 - core) * MIDDLE, 32), 256)
    mine = finish((1 - core) * MIDDLE, 256)
    other = acc_mid[...] + jnp.dot(leg_x[middle, :], rows_x[1 - core], preferred_element_type=F32)
    merged = jnp.where(own_mid[...] == 1, mine, other).astype(BF16)

    @pl.when(core == 0)
    def _():
        place(MIDDLE, SHARE - MIDDLE, merged[: SHARE - MIDDLE], 0)

    @pl.when(core == 1)
    def _():
        last = MIDDLE + UPPER + rows_iota((SPAN - UPPER, 1)) < TOTAL
        ending = finish(UPPER, SPAN - UPPER)
        ready[MIDDLE + 32 : MIDDLE + 48, :] = jnp.where(last, ending, jnp.zeros_like(ending)).astype(BF16)
        ready[MIDDLE + 48 : SHARE, :] = jnp.zeros((SHARE - MIDDLE - 48, 256), BF16)
        ready[0:32, :] = merged[SHARE - MIDDLE :]
        pltpu.make_async_copy(ready.at[0:32], out.at[0:32], sem.at[0]).start()
        pltpu.make_async_copy(ready.at[MIDDLE + 32 : SHARE], out.at[MIDDLE + 32 : SHARE], sem.at[0]).start()

    for i in range(MIDDLE // BLOCK):
        value = finish(core * 256 + i * BLOCK, BLOCK).astype(BF16)
        copies.append(place(core * 32 + i * BLOCK, BLOCK, value, 1 + i))
    for copy in copies:
        copy.wait()
    pltpu.make_async_copy(ready.at[MIDDLE:SHARE], out.at[MIDDLE:SHARE], sem.at[0]).wait()


def shards(spectra, legendre, weights, coefficient, row_length, wave_number):
    message = pltpu.VMEM((2, CHIPS, 8, 128), BF16)
    vmem = pl.BlockSpec(memory_space=pltpu.VMEM)
    hbm = pl.BlockSpec(memory_space=pltpu.HBM)
    dma = pltpu.SemaphoreType.DMA
    kept = pl.pallas_call(
        couple_kernel,
        out_shape=[
            pltpu.VMEM((SPAN, 256), F32),
            pltpu.VMEM((256, 256), F32),
            pltpu.VMEM((SPAN, 512), BF16),
            pltpu.VMEM((2, 512, 256), BF16),
            pltpu.VMEM((256, 256), jnp.int32),
        ],
        in_specs=[hbm] * 6,
        out_specs=[vmem] * 5,
        scratch_shapes=[
            pltpu.SMEM((1, 4), F32),
            pltpu.VMEM((1, 4, 2, 2 * BAND - 1), F32),
            pltpu.SMEM((1, 4), jnp.int32),
            pltpu.SMEM((2,), jnp.int32),
            pltpu.VMEM((ROWS, 512), BF16),
            pltpu.VMEM((UPPER, 256), BF16),
            pltpu.VMEM((SPAN, 256), BF16),
            message, message, message, message, message,
            pltpu.VMEM((CHIPS * 8, 128), F32),
            pltpu.VMEM((8, 2 * BAND), F32),
            pltpu.VMEM((4, 2, BAND, BAND), BF16),
            pltpu.VMEM((NZ, 128), jnp.int32),
            pltpu.VMEM((NZ - 1, NZ, 128), jnp.int32),
            pltpu.VMEM((NZ, 128), jnp.int32),
            pltpu.VMEM((NY, NZ, 128), jnp.int32),
            pltpu.VMEM((NY * NZ, 128), jnp.int32),
            pltpu.VMEM((NX, NY * NZ, 128), jnp.int32),
            pltpu.VMEM((2, 512, 256), BF16),
            dma((2 + 2 * NX,)), dma((4,)), dma((2,)), dma((2,)), dma((2,)), dma((2,)),
            dma((3,)), dma((3,)), dma((3,)), dma((3,)),
        ],
        compiler_params=pltpu.CompilerParams(
            collective_id=0, has_side_effects=True, vmem_limit_bytes=48 * 1024 * 1024
        ),
        name="transforms",
    )(spectra, legendre, weights, coefficient, row_length, wave_number)
    return pl.pallas_call(
        finish_kernel,
        out_shape=jax.ShapeDtypeStruct((SHARE, 256), BF16),
        in_specs=[vmem] * 5,
        out_specs=hbm,
        scratch_shapes=[pltpu.VMEM((SHARE, 256), BF16), dma((1 + MIDDLE // BLOCK,))],
        compiler_params=pltpu.CompilerParams(vmem_limit_bytes=48 * 1024 * 1024),
        name="finish",
    )(*[pltpu.with_memory_space_constraint(a, pltpu.VMEM) for a in kept])


def solution(mesh):
    return jax.shard_map(
        shards,
        mesh=mesh,
        in_specs=(
            P("wide", None),
            P("wide", "narrow"),
            P("narrow", "wide"),
            P("narrow", "wide", None, None),
            P("narrow", "wide"),
            P("wide"),
        ),
        out_specs=P(("wide", "narrow"), None),
        check_vma=False,
    )
```

```python
import functools

import jax
import jax.numpy as jnp
from jax import lax
from jax.experimental import pallas as pl
from jax.experimental.pallas import tpu as pltpu
from jax.sharding import PartitionSpec as P

TRUNC = 3999
NX, NY, NZ = 4, 4, 8
CHIPS = NX * NY * NZ
BAND = 2 * CHIPS
MIDDLE = 3744
UPPER = TRUNC + 1
TOTAL = 2 * TRUNC + 3 - BAND
SPAN = 4016
ROWS = MIDDLE + SPAN
SHARE = 3968
BLOCK = 416
Z_ORDER = (0, 3, 1, 2, 4, 7, 5, 6)
MESH = pl.DeviceIdType.MESH
BF16, F32 = jnp.bfloat16, jnp.float32
ROW_ROW = (((0,), (0,)), ((), ()))


def rows_iota(shape):
    return lax.broadcasted_iota(jnp.int32, shape, 0)


def swap_blocks(a, b, c, d, sizes):
    place = rows_iota(a.shape) % 8
    n = a.shape[0]
    for size in sizes:
        keep = place % (2 * size) < size

        def trade(p, q):
            return jnp.where(keep, p, pltpu.roll(q, size, 0)), jnp.where(keep, pltpu.roll(p, n - size, 0), q)

        if size == 4:
            a, c = trade(a, c)
            b, d = trade(b, d)
        else:
            a, b = trade(a, b)
            c, d = trade(c, d)
    return a, b, c, d


def couple_kernel(
    spectra, legendre, weights_in, coef_in, lengths_in, waves_in, acc, acc_mid, leg_x1, rows_x, own_mid,
    weights, coef, lengths, waves, leg, spec_a, spec_b, send, recv, send_back, recv_back, from_pair, grid, harm, table,
    leg_x, leg_own, leg_x0, perm,
    block_z, from_z, block_y, from_y, block_x, from_x, rows,
    load_sem, small_sem, send_sem, recv_sem, back_send_sem, back_recv_sem, wave_send, wave_recv,
    pair_send, pair_recv,
):
    me = lax.axis_index("wide")
    core = lax.axis_index("narrow")
    my_z, my_y, my_x = me % NZ, (me // NZ) % NY, me // (NZ * NY)

    def push(src, dst, sem_out, sem_in, chip, on_core=core):
        return pltpu.make_async_remote_copy(
            src_ref=src, dst_ref=dst, send_sem=sem_out, recv_sem=sem_in,
            device_id=(chip, on_core), device_id_type=MESH,
        )

    small = [
        pltpu.make_async_copy(src, dst, small_sem.at[i])
        for i, (src, dst) in enumerate(
            [(waves_in, waves), (lengths_in, lengths), (weights_in, weights), (coef_in, coef)]
        )
    ]
    loads = [
        pltpu.make_async_copy(spectra.at[pl.ds(0, UPPER)], spec_a, load_sem.at[0]),
        pltpu.make_async_copy(spectra.at[pl.ds(MIDDLE, SPAN)], spec_b, load_sem.at[1]),
    ]

    def chunk_of(step):
        return (my_x + step) % NX

    def load_leg(step, part):
        lanes = pl.ds(pl.multiple_of(chunk_of(step) * 128, 128), 128)
        span = pl.ds(0, UPPER) if part == 0 else pl.ds(UPPER, ROWS - UPPER)
        return pltpu.make_async_copy(
            legendre.at[span, lanes], leg.at[span, lanes], load_sem.at[2 + 2 * step + part]
        )

    small[0].start()
    loads[0].start()
    load_leg(0, 0).start()
    loads[1].start()
    load_leg(0, 1).start()
    for copy in small[1:]:
        copy.start()

    barrier = pltpu.get_barrier_semaphore()

    def greet(i, carry):
        pl.semaphore_signal(
            barrier, inc=1, device_id=(lax.rem(me + i, CHIPS), core), device_id_type=MESH
        )
        return carry

    lax.fori_loop(1, CHIPS, greet, 0, unroll=8)
    pl.semaphore_signal(barrier, inc=1, device_id=(me, 1 - core), device_id_type=MESH)

    small[0].wait()
    first = waves[0]
    in_first = (MIDDLE + rows_iota((256, 256)) < UPPER - first).astype(jnp.int32)
    own_mid[...] = jnp.where(in_first == 1 - core, 1, 0)
    block_z[...] = jnp.where(rows_iota((NZ, 128)) == my_z, first, 0)

    def inverse(step):
        lanes = pl.ds(pl.multiple_of(chunk_of(step) * 128, 128), 128)
        if step == 0:
            loads[0].wait()
            load_leg(1, 0).start()
            middle = MIDDLE + rows_iota((UPPER - MIDDLE, 1))
            own = middle < UPPER - first
            here = spec_a[MIDDLE:UPPER, :]
            spec_a[MIDDLE:UPPER, :] = jnp.where(own, here, jnp.zeros_like(here))
        load_leg(step, 0).wait()
        if step == 0:
            load_leg(1, 1).start()
        elif step < 3:
            load_leg(step + 1, 1).start()
        wave_a = lax.dot_general(leg[0:UPPER, lanes], spec_a[...], ROW_ROW, preferred_element_type=F32)
        if step == 0:
            loads[1].wait()
            load_leg(2, 0).start()
            here = spec_b[0 : UPPER - MIDDLE, :]
            spec_b[0 : UPPER - MIDDLE, :] = jnp.where(own, jnp.zeros_like(here), here)
            here = spec_b[UPPER:SPAN, :]
            tail = MIDDLE + UPPER + rows_iota((SPAN - UPPER, 1)) < TOTAL
            spec_b[UPPER:SPAN, :] = jnp.where(tail, here, jnp.zeros_like(here))
        load_leg(step, 1).wait()
        if step == 1:
            load_leg(3, 0).start()
        wave_b = lax.dot_general(leg[MIDDLE:ROWS, lanes], spec_b[...], ROW_ROW, preferred_element_type=F32)
        even0, even1, odd0, odd1 = swap_blocks(
            wave_a[:, :128], wave_a[:, 128:], wave_b[:, :128], wave_b[:, 128:], (4, 2)
        )
        for c, (even, odd) in enumerate(((even0, odd0), (even1, odd1))):
            both = jnp.stack([even.reshape(16, 8, 128), odd.reshape(16, 8, 128)], axis=1)
            send[c, pl.ds(chunk_of(step) * 32, 32)] = both.reshape(32, 8, 128).astype(BF16)

    def push_chunk(c, step):
        for dy in range(NY):
            line = (chunk_of(step) * NY + lax.rem(my_y + dy, NY)) * NZ

            def one(i, carry):
                chip = line + lax.rem(my_z + i, NZ)
                push(send.at[c, chip], recv.at[c, me], send_sem.at[c], recv_sem.at[c], chip).start()
                return carry

            lax.fori_loop(1 if step == 0 and dy == 0 else 0, NZ, one, 0, unroll=4)

    def z_push(d):
        chip = (my_x * NY + my_y) * NZ + (my_z + d) % NZ
        return push(block_z, from_z.at[d - 1], wave_send.at[0], wave_recv.at[0], chip)

    def y_push(d):
        chip = (my_x * NY + (my_y + d) % NY) * NZ + my_z
        return push(block_y, from_y.at[my_y], wave_send.at[1], wave_recv.at[1], chip)

    def x_push(d):
        chip = (((my_x + d) % NX) * NY + my_y) * NZ + my_z
        return push(block_x, from_x.at[my_x], wave_send.at[2], wave_recv.at[2], chip)

    inverse(0)
    pl.semaphore_wait(barrier, CHIPS)
    for d in range(1, NZ):
        z_push(d).start()
    push_chunk(0, 0)
    inverse(1)
    push_chunk(0, 1)
    inverse(2)
    push_chunk(0, 2)
    inverse(3)
    push_chunk(0, 3)
    pltpu.make_async_copy(from_z, from_z, wave_recv.at[0]).wait()
    block_y[...] = block_z[...] + jnp.sum(from_z[...], axis=0)
    from_y[my_y] = block_y[...]
    for d in range(1, NY):
        y_push(d).start()
    for step in range(NX):
        push_chunk(1, step)
    for c in range(2):
        recv[c, me] = send[c, me]
    pltpu.make_async_copy(from_y.at[pl.ds(0, NY - 1)], from_y.at[pl.ds(0, NY - 1)], wave_recv.at[1]).wait()
    block_x[...] = from_y[...].reshape(NY * NZ, 128)
    from_x[my_x] = block_x[...]
    for d in range(1, NX):
        x_push(d).start()

    for copy in small[1:]:
        copy.wait()
    harm[...] = jnp.zeros_like(harm)
    for l in range(4):
        for part in range(2):
            harm[pl.ds(2 * l + part, 1), 0 : BAND * 2 - 1] = coef[0, l, pl.ds(part, 1), :]
    for l in range(4):
        for part in range(2):
            line = jnp.broadcast_to(harm[pl.ds(2 * l + part, 1), :], (BAND, 2 * BAND))
            turned = pltpu.roll(line, BAND + 1, 1, stride=1, stride_axis=0)
            table[l, part] = turned[:, :BAND].astype(BF16)

    pltpu.make_async_copy(from_x.at[pl.ds(0, NX - 1)], from_x.at[pl.ds(0, NX - 1)], wave_recv.at[2]).wait()
    wave = from_x[...].reshape(CHIPS, 128)
    wave = jnp.concatenate([wave, wave], axis=1)
    falling = BAND - 1 - lax.broadcasted_iota(jnp.int32, (CHIPS, BAND), 1)
    picks = jnp.concatenate(
        [jnp.where(wave == falling, 1.0, 0.0), jnp.where(BAND - 1 - wave == falling, 1.0, 0.0)], axis=0
    ).astype(BF16)
    number = BAND - 1 - rows_iota((BAND, 1))

    def arrival(buffer, c, sem):
        part = buffer.at[c, pl.ds(0, CHIPS - 1)]
        return pltpu.make_async_copy(part, part, sem.at[c])

    def couple(c):
        arrival(recv, c, recv_sem).wait()
        grid[...] = recv[c].astype(F32).reshape(CHIPS * 8, 128)
        columns = []
        for l in range(2):
            for part in range(2):
                columns.append(
                    jnp.concatenate(
                        [grid[pl.ds(slot * 4 + part * 2 + l, CHIPS, stride=8), :] for slot in range(2)], axis=0
                    )
                )
        by_slot = jnp.concatenate(columns, axis=1).astype(BF16)
        natural = lax.dot_general(picks, by_slot, ROW_ROW, preferred_element_type=F32)
        scaled = []
        for l in range(2):
            row = 2 * c + l
            resolved = number < lengths[0, row]
            here = natural[:, 256 * l : 256 * l + 256]
            masked = jnp.where(resolved, here, jnp.zeros_like(here)).astype(BF16)
            real = jnp.dot(table[row, 0], masked, preferred_element_type=F32)
            imag = jnp.dot(table[row, 1], masked, preferred_element_type=F32)
            coupled = jnp.concatenate(
                [real[:, :128] - imag[:, 128:], real[:, 128:] + imag[:, :128]], axis=1
            )
            coupled = coupled * weights[0, row]
            scaled.append(jnp.where(resolved, coupled, jnp.zeros_like(coupled)).astype(BF16))
        by_slot = jnp.dot(picks, jnp.concatenate(scaled, axis=1), preferred_element_type=F32)
        for l in range(2):
            for part in range(2):
                lanes = slice((2 * l + part) * 128, (2 * l + part) * 128 + 128)
                for slot in range(2):
                    grid[pl.ds(slot * 4 + part * 2 + l, CHIPS, stride=8), :] = by_slot[
                        slot * CHIPS : slot * CHIPS + CHIPS, lanes
                    ]
        send_back[c] = grid[...].reshape(CHIPS, 8, 128).astype(BF16)

        def push_back(chip):
            push(
                send_back.at[c, chip], recv_back.at[c, me], back_send_sem.at[c], back_recv_sem.at[c], chip
            ).start()

        for z in Z_ORDER:

            def one(i, carry):
                push_back((lax.rem(my_x + i // NY, NX) * NY + lax.rem(my_y + i, NY)) * NZ + z)
                return carry

            lax.fori_loop(1, NX * NY, one, 0, unroll=5)

            @pl.when(my_z != z)
            def _():
                push_back((my_x * NY + my_y) * NZ + z)

        recv_back[c, me] = send_back[c, me]

    new = lax.broadcasted_iota(jnp.int32, (256, 256), 1)
    old = ((new & 127) >> 1) * 4 + (new >> 7) * 2 + (new & 1)
    perm[...] = jnp.where(rows_iota((256, 256)) == old, 1.0, 0.0).astype(BF16)

    def in_order(lines):
        left, right = [
            jnp.dot(part, perm[...], preferred_element_type=F32).astype(BF16)
            for part in (lines[:, :256], lines[:, 256:])
        ]
        return (
            jnp.concatenate([left[:, :128], right[:, :128]], axis=1),
            jnp.concatenate([left[:, 128:], right[:, 128:]], axis=1),
        )

    blocks = [(start, min(BLOCK, SPAN - start)) for start in range(0, SPAN, BLOCK)]

    theirs = pl.ds(pl.multiple_of((1 - core) * MIDDLE, 32), SPAN)
    leg_push = push(leg.at[theirs], leg_x, pair_send.at[0], pair_recv.at[0], me, 1 - core)
    leg_push.start()
    couple(0)
    couple(1)
    for start, size in blocks:
        own = leg[pl.ds(pl.multiple_of(core * MIDDLE + start, 16), size), :]
        leg_own[start : start + size, :256], leg_own[start : start + size, 256:] = in_order(own)
    leg_push.wait_recv()
    for start, size in blocks:
        span = slice(start, start + size)
        leg_x0[span, :], leg_x1[span, :] = in_order(leg_x[span, :])

    def swap(c):
        return push(recv_back.at[c], from_pair.at[c], pair_send.at[1 + c], pair_recv.at[1 + c], me, 1 - core)

    def by_latitude(buffer, c, target):
        parts = buffer[c].astype(F32).reshape(CHIPS // 4, 4, 8, 128)
        real_a, imag_a, real_b, imag_b = swap_blocks(
            *[parts[:, i].reshape(2 * CHIPS, 128) for i in range(4)], (4, 2)
        )
        target[0] = jnp.concatenate([real_a, imag_a], axis=1).astype(BF16)
        target[1] = jnp.concatenate([real_b, imag_b], axis=1).astype(BF16)

    shared = pl.ds(pl.multiple_of((1 - core) * MIDDLE, 32), 256)

    arrival(recv_back, 0, back_recv_sem).wait()
    swap(0).start()
    by_latitude(recv_back, 0, rows)
    swap(0).wait_recv()
    by_latitude(from_pair, 0, rows_x)
    for start, size in blocks:
        span = slice(start, start + size)
        acc[span, :] = jnp.dot(leg_own[span, :256], rows[core], preferred_element_type=F32) + jnp.dot(
            leg_x0[span, :], rows_x[core], preferred_element_type=F32
        )
    acc_mid[...] = jnp.dot(leg_own[shared, :256], rows[1 - core], preferred_element_type=F32) + jnp.dot(
        leg_x0[shared, :], rows_x[1 - core], preferred_element_type=F32
    )

    arrival(recv_back, 1, back_recv_sem).wait()
    swap(1).start()
    by_latitude(recv_back, 1, rows)
    for start, size in blocks:
        span = slice(start, start + size)
        acc[span, :] += jnp.dot(leg_own[span, 256:], rows[core], preferred_element_type=F32)
    acc_mid[...] += jnp.dot(leg_own[shared, 256:], rows[1 - core], preferred_element_type=F32)

    for d in range(1, NZ):
        z_push(d).wait_send()
    for d in range(1, NY):
        y_push(d).wait_send()
    for d in range(1, NX):
        x_push(d).wait_send()
    for c in range(2):
        arrival(recv, c, send_sem).wait()
        arrival(recv_back, c, back_send_sem).wait()
    leg_push.wait_send()
    swap(0).wait_send()
    swap(1).wait()
    by_latitude(from_pair, 1, rows_x)


def finish_kernel(acc, acc_mid, leg_x, rows_x, own_mid, out, ready, sem):
    core = lax.axis_index("narrow")
    copies = []

    def place(start, size, value, i):
        span = pl.ds(pl.multiple_of(start, 16), size)
        ready[span, :] = value
        copy = pltpu.make_async_copy(ready.at[span], out.at[span], sem.at[i])
        copy.start()
        return copy

    def finish(start, size):
        span = pl.ds(pl.multiple_of(start, 16), size)
        return acc[span, :] + jnp.dot(leg_x[span, :], rows_x[core], preferred_element_type=F32)

    middle = pl.ds(pl.multiple_of((1 - core) * MIDDLE, 32), 256)
    mine = finish((1 - core) * MIDDLE, 256)
    other = acc_mid[...] + jnp.dot(leg_x[middle, :], rows_x[1 - core], preferred_element_type=F32)
    merged = jnp.where(own_mid[...] == 1, mine, other).astype(BF16)

    @pl.when(core == 0)
    def _():
        place(MIDDLE, SHARE - MIDDLE, merged[: SHARE - MIDDLE], 0)

    @pl.when(core == 1)
    def _():
        last = MIDDLE + UPPER + rows_iota((SPAN - UPPER, 1)) < TOTAL
        ending = finish(UPPER, SPAN - UPPER)
        ready[MIDDLE + 32 : MIDDLE + 48, :] = jnp.where(last, ending, jnp.zeros_like(ending)).astype(BF16)
        ready[MIDDLE + 48 : SHARE, :] = jnp.zeros((SHARE - MIDDLE - 48, 256), BF16)
        ready[0:32, :] = merged[SHARE - MIDDLE :]
        pltpu.make_async_copy(ready.at[0:32], out.at[0:32], sem.at[0]).start()
        pltpu.make_async_copy(ready.at[MIDDLE + 32 : SHARE], out.at[MIDDLE + 32 : SHARE], sem.at[0]).start()

    for i in range(MIDDLE // BLOCK):
        value = finish(core * 256 + i * BLOCK, BLOCK).astype(BF16)
        copies.append(place(core * 32 + i * BLOCK, BLOCK, value, 1 + i))
    for copy in copies:
        copy.wait()
    pltpu.make_async_copy(ready.at[MIDDLE:SHARE], out.at[MIDDLE:SHARE], sem.at[0]).wait()


def shards(spectra, legendre, weights, coefficient, row_length, wave_number):
    message = pltpu.VMEM((2, CHIPS, 8, 128), BF16)
    vmem = pl.BlockSpec(memory_space=pltpu.VMEM)
    hbm = pl.BlockSpec(memory_space=pltpu.HBM)
    dma = pltpu.SemaphoreType.DMA
    kept = pl.pallas_call(
        couple_kernel,
        out_shape=[
            pltpu.VMEM((SPAN, 256), F32),
            pltpu.VMEM((256, 256), F32),
            pltpu.VMEM((SPAN, 256), BF16),
            pltpu.VMEM((2, 256, 256), BF16),
            pltpu.VMEM((256, 256), jnp.int32),
        ],
        in_specs=[hbm] * 6,
        out_specs=[vmem] * 5,
        scratch_shapes=[
            pltpu.SMEM((1, 4), F32),
            pltpu.VMEM((1, 4, 2, 2 * BAND - 1), F32),
            pltpu.SMEM((1, 4), jnp.int32),
            pltpu.SMEM((2,), jnp.int32),
            pltpu.VMEM((ROWS, 512), BF16),
            pltpu.VMEM((UPPER, 256), BF16),
            pltpu.VMEM((SPAN, 256), BF16),
            message, message, message, message, message,
            pltpu.VMEM((CHIPS * 8, 128), F32),
            pltpu.VMEM((8, 2 * BAND), F32),
            pltpu.VMEM((4, 2, BAND, BAND), BF16),
            pltpu.VMEM((SPAN, 512), BF16),
            pltpu.VMEM((SPAN, 512), BF16),
            pltpu.VMEM((SPAN, 256), BF16),
            pltpu.VMEM((256, 256), BF16),
            pltpu.VMEM((NZ, 128), jnp.int32),
            pltpu.VMEM((NZ - 1, NZ, 128), jnp.int32),
            pltpu.VMEM((NZ, 128), jnp.int32),
            pltpu.VMEM((NY, NZ, 128), jnp.int32),
            pltpu.VMEM((NY * NZ, 128), jnp.int32),
            pltpu.VMEM((NX, NY * NZ, 128), jnp.int32),
            pltpu.VMEM((2, 256, 256), BF16),
            dma((2 + 2 * NX,)), dma((4,)), dma((2,)), dma((2,)), dma((2,)), dma((2,)),
            dma((3,)), dma((3,)), dma((3,)), dma((3,)),
        ],
        compiler_params=pltpu.CompilerParams(
            collective_id=0, has_side_effects=True, vmem_limit_bytes=48 * 1024 * 1024
        ),
        name="transforms",
    )(spectra, legendre, weights, coefficient, row_length, wave_number)
    return pl.pallas_call(
        finish_kernel,
        out_shape=jax.ShapeDtypeStruct((SHARE, 256), BF16),
        in_specs=[vmem] * 5,
        out_specs=hbm,
        scratch_shapes=[pltpu.VMEM((SHARE, 256), BF16), dma((1 + MIDDLE // BLOCK,))],
        compiler_params=pltpu.CompilerParams(vmem_limit_bytes=48 * 1024 * 1024),
        name="finish",
    )(*[pltpu.with_memory_space_constraint(a, pltpu.VMEM) for a in kept])


def solution(mesh):
    return jax.shard_map(
        shards,
        mesh=mesh,
        in_specs=(
            P("wide", None),
            P("wide", "narrow"),
            P("narrow", "wide"),
            P("narrow", "wide", None, None),
            P("narrow", "wide"),
            P("wide"),
        ),
        out_specs=P(("wide", "narrow"), None),
        check_vma=False,
    )
```
